32 devices in a mesh: batch: 8 (over z, y), span: 4 (over x, core).
Axes of the slice: x: 2, y: 2, z: 4, core: 2. Of those that a mesh axis runs over, the one named last changes fastest.
Arguments:
- image_embeds: float32 [4096, 768], P(('batch', 'span')), may hold values from -1.2 to 1.2
- text_embeds: float32 [4096, 768], P(('batch', 'span')), may hold values from -1.2 to 1.2
Outputs:
- image_lse: float32 [4096], P(('batch', 'span'))
- text_lse: float32 [4096], P(('batch', 'span'))
- image_grad: float32 [4096, 768], P(('batch', 'span'))
- text_grad: float32 [4096, 768], P(('batch', 'span'))
The draws below stay inside these ranges and needn't reach their ends.
All inputs are finite; a program needn't handle non-finite values.
Results may differ from the reference program's by a relative error of at most 0.0051.
Values may be sent and summed in bfloat16 or wider, within the bound.
No kernel may reach another device: no remote copies, remote signals or barrier semaphores. Data moves between devices by JAX's collectives and lax.ppermute only.
A program may use at most 64 MiB of HBM per device.

```python
import jax
import jax.numpy as jnp
from jax import lax

E = 768
STEPS = 4
BLOCK = 512
N_SAMPLES = 4096
N_BATCH = 8


def pair_pattern(key):
    amplitude = (10.0 / E) ** 0.5
    half = jnp.where(jax.random.bernoulli(key, 0.5, (N_SAMPLES // 2, E)), amplitude, -amplitude)
    return jnp.repeat(half, 2, axis=0)


def planted(mixed, pattern, base):
    rows = jnp.arange(N_SAMPLES)[:, None]
    strength = 1.0 + 0.4 * (rows // 64 % 4).astype(jnp.float32)
    height = 50.0 * strength * strength
    offset = 2.0 / height
    aligned = strength * (1.0 + offset * (rows % 2).astype(jnp.float32)) * pattern + 0.05 * base
    return jnp.clip(jnp.where(rows % 64 < 2, aligned, mixed), -1.2, 1.2)


def draw_image_embeds(key, part):
    pattern = pair_pattern(key)
    key = jax.random.fold_in(key, 1)
    base = jax.random.truncated_normal(key, -6.0, 6.0, (N_SAMPLES, E)) * 0.1
    return planted(base, pattern, base)


def draw_text_embeds(key, part):
    pattern = pair_pattern(key)
    key = jax.random.fold_in(key, 2)
    base = jax.random.truncated_normal(key, -6.0, 6.0, (N_SAMPLES, E)) * 0.1
    return planted(base, pattern, base)


def setup_inputs(seed: int = 0) -> dict:
    splits = jax.random.split(jax.random.key(seed), 3)
    return {
        "image_embeds": draw_image_embeds(jax.random.fold_in(splits[2], 71), 0),
        "text_embeds": draw_text_embeds(jax.random.fold_in(splits[2], 71), 0),
    }


LOGIT_SCALE = 5.0


def reference(image_embeds, text_embeds):
    image_b = image_embeds.astype(jnp.bfloat16).reshape(N_BATCH, BLOCK, E).astype(jnp.float32)
    text_b = text_embeds.astype(jnp.bfloat16).reshape(N_BATCH, BLOCK, E).astype(jnp.float32)
    scores = []
    for step in range(STEPS):
        moved = jnp.roll(text_b, step, axis=0)
        scores.append(jnp.einsum("aie,aje->aij", image_b, moved) * LOGIT_SCALE)
    stacked = jnp.stack(scores, 1)
    image_lse = jax.nn.logsumexp(stacked, axis=(1, 3))
    column_stack = jnp.stack([jnp.roll(scores[step], -step, axis=0) for step in range(STEPS)], 1)
    text_lse = jax.nn.logsumexp(column_stack, axis=(1, 2))
    eye_block = jnp.eye(BLOCK, dtype=jnp.float32)
    image_grad = jnp.zeros((N_BATCH, BLOCK, E), jnp.float32)
    text_grad = jnp.zeros((N_BATCH, BLOCK, E), jnp.float32)
    for step in range(STEPS):
        current = scores[step]
        lse_cols = jnp.roll(text_lse, step, axis=0)
        weights = 0.5 * jnp.exp(current - image_lse[:, :, None]) + 0.5 * jnp.exp(current - lse_cols[:, None, :])
        if step == 0:
            weights = weights - eye_block[None, :, :]
        rounded = lax.optimization_barrier(weights.astype(jnp.bfloat16)).astype(jnp.float32)
        moved = jnp.roll(text_b, step, axis=0)
        image_grad = image_grad + LOGIT_SCALE * jnp.einsum("aij,aje->aie", rounded, moved)
        partial_text = LOGIT_SCALE * jnp.einsum("aij,aie->aje", rounded, image_b)
        text_grad = text_grad + jnp.roll(partial_text, -step, axis=0)
    return (image_lse.reshape(N_SAMPLES), text_lse.reshape(N_SAMPLES),
            image_grad.reshape(N_SAMPLES, E), text_grad.reshape(N_SAMPLES, E))
```

```python
import jax
import jax.numpy as jnp
from jax import lax
from jax.sharding import PartitionSpec as P

STEPS = 4
LOGIT_SCALE = 5.0
AXES = ("batch", "span")


def moved(value, target):
    count, spans = lax.axis_size("batch"), lax.axis_size("span")
    pairs = []
    for b in range(count):
        for s in range(spans):
            to_b, to_s = target(b, s)
            pairs.append((b * spans + s, (to_b % count) * spans + to_s))
    return lax.ppermute(value, AXES, pairs)


def over_core(value):
    return moved(value, lambda b, s: (b, s ^ 1))


def over_x(value):
    return moved(value, lambda b, s: (b, s ^ 2))


def along(value, steps):
    return moved(value, lambda b, s: (b + steps, s))


def scores_of(rows, cols):
    return (
        lax.dot_general(rows, cols, (((1,), (1,)), ((), ())), preferred_element_type=jnp.float32)
        * LOGIT_SCALE
    )


def partial_lse(rows, cols):
    scores = [scores_of(rows, col) for col in cols]
    top = scores[0].max(axis=1)
    for s in scores[1:]:
        top = jnp.maximum(top, s.max(axis=1))
    total = 0.0
    for s in scores:
        total = total + jnp.sum(jnp.exp(s - top[:, None]), axis=1)
    return top + jnp.log(total)


def relative(pieces, span_pos):
    shape = pieces.shape
    p = pieces.reshape(shape[:-2] + (2, 2) + shape[-1:])
    p = jnp.where(span_pos // 2 == 1, jnp.flip(p, -3), p)
    p = jnp.where(span_pos % 2 == 1, jnp.flip(p, -2), p)
    return p.reshape(shape)


def gradient(rows, cols, row_lse, col_lse):
    total = 0.0
    for k, (col, lse) in enumerate(zip(cols, col_lse)):
        s = scores_of(rows, col)
        w = 0.5 * jnp.exp(s - row_lse[:, None]) + 0.5 * jnp.exp(s - lse[None, :])
        if k == 0:
            n = rows.shape[0] // 2
            i = lax.broadcasted_iota(jnp.int32, s.shape, 0)
            j = lax.broadcasted_iota(jnp.int32, s.shape, 1)
            w = w - ((i == j) & (i < n)).astype(jnp.float32)
        w = w.astype(jnp.bfloat16)
        total = total + LOGIT_SCALE * jnp.dot(w, col, preferred_element_type=jnp.float32)
    return total


def all_lse(part):
    count, spans = lax.axis_size("batch"), lax.axis_size("span")
    n = part.shape[-1]
    send = jnp.broadcast_to(part[None], (count * spans,) + part.shape)
    got = lax.all_to_all(send, AXES, 0, 0, tiled=True).reshape((count, spans) + part.shape)
    out = []
    for piece in range(4):
        terms = [got[:, s, :, piece ^ s] for s in range(4)]
        top = jnp.maximum(jnp.maximum(terms[0], terms[1]), jnp.maximum(terms[2], terms[3]))
        out.append(top + jnp.log(sum(jnp.exp(t - top) for t in terms)))
    return jnp.stack(out, 2)


def body(image_embeds, text_embeds):
    i0 = image_embeds.astype(jnp.bfloat16)
    t0 = text_embeds.astype(jnp.bfloat16)
    rows = i0.shape[0]
    pos = lax.axis_index("span")
    b = lax.axis_index("batch")
    texts = [t0] + [along(t0, k) for k in range(1, STEPS)]
    images = [i0] + [along(i0, -k) for k in range(1, STEPS)]
    texts_x = [over_x(v) for v in texts]
    images_x = [over_x(v) for v in images]
    ct0, ci0 = over_core(t0), over_core(i0)
    cxt0, cxi0 = over_core(texts_x[0]), over_core(images_x[0])
    image_rows = jnp.concatenate([i0, ci0, images_x[0], cxi0])
    text_rows = jnp.concatenate([t0, ct0, texts_x[0], cxt0])
    part = jnp.stack([partial_lse(image_rows, texts), partial_lse(text_rows, images)])
    lse = relative(all_lse(part.reshape(2, 4, rows)), pos)
    count = lse.shape[0]
    around = jnp.concatenate([lse, lse])
    image_lses = lax.dynamic_slice_in_dim(around[:, 0], b, STEPS)
    text_lses = lax.dynamic_slice_in_dim(around[:, 1], b + count - (STEPS - 1), STEPS)[::-1]
    own_image = image_lses[0, :2].reshape(2 * rows)
    own_text = text_lses[0, :2].reshape(2 * rows)

    def cols(a, ax):
        return [jnp.concatenate([v, w]) for v, w in zip(a, ax)]

    def col_lse(l):
        return [jnp.concatenate([l[k, 0], l[k, 2]]) for k in range(STEPS)]

    grad_i = gradient(image_rows[: 2 * rows], cols(texts, texts_x), own_image, col_lse(text_lses))
    grad_t = gradient(text_rows[: 2 * rows], cols(images, images_x), own_text, col_lse(image_lses))
    image_grad = grad_i[:rows] + over_core(grad_i[rows:])
    text_grad = grad_t[:rows] + over_core(grad_t[rows:])
    return (own_image[:rows], own_text[:rows], image_grad, text_grad)


def solution(mesh):
    in_specs = (P(("batch", "span"), None), P(("batch", "span"), None))
    out_specs = (
        P(("batch", "span")),
        P(("batch", "span")),
        P(("batch", "span"), None),
        P(("batch", "span"), None),
    )
    return jax.shard_map(body, mesh=mesh, in_specs=in_specs, out_specs=out_specs, check_vma=False)
```

```python
import functools

import jax
import jax.numpy as jnp
from jax import lax
from jax.experimental import pallas as pl
from jax.experimental.pallas import tpu as pltpu
from jax.sharding import PartitionSpec as P

STEPS = 4
LOGIT_SCALE = 5.0
AXES = ("batch", "span")
SPANS = 4
F32, BF16 = jnp.float32, jnp.bfloat16
VMEM_LIMIT = 32 * 1024 * 1024


def moved(value, target):
    count, spans = lax.axis_size("batch"), lax.axis_size("span")
    pairs = []
    for b in range(count):
        for s in range(spans):
            to_b, to_s = target(b, s)
            pairs.append((b * spans + s, (to_b % count) * spans + to_s))
    return lax.ppermute(value, AXES, pairs)


def over_core(value):
    return moved(value, lambda b, s: (b, s ^ 1))


def over_x(value):
    return moved(value, lambda b, s: (b, s ^ 2))


def along(value, steps):
    return moved(value, lambda b, s: (b + steps, s))


def dot_t(a, b):
    return lax.dot_general(a, b, (((1,), (1,)), ((), ())), preferred_element_type=F32)


def call(kernel, out_shape, scratch, flops, *args):
    whole = pl.BlockSpec(memory_space=pltpu.VMEM)
    size = sum(a.size * a.dtype.itemsize for a in args)
    return pl.pallas_call(
        kernel,
        out_shape=out_shape,
        in_specs=[whole] * len(args),
        out_specs=jax.tree.map(lambda _: whole, out_shape),
        scratch_shapes=scratch,
        compiler_params=pltpu.CompilerParams(vmem_limit_bytes=VMEM_LIMIT),
        cost_estimate=pl.CostEstimate(flops=flops, bytes_accessed=size, transcendentals=0),
    )(*args)


def cast_kernel(image, text, i_out, t_out, own):
    i = image[...].astype(BF16)
    t = text[...].astype(BF16)
    n = i.shape[0]
    i_out[...] = i
    t_out[...] = t
    own[:n] = t
    own[n:] = i


def stats_kernel(count, *refs):
    own, core, x, corex, t1, t2, t3, i1, i2, i3, out, rows, cols = refs
    n = t1.shape[0]
    pos = lax.axis_index("span")
    near = (own, core, x, corex)
    part = []
    for side in range(2):
        for q, ref in enumerate(near):
            rows[side, q * n : (q + 1) * n] = ref[n:] if side == 0 else ref[:n]
        cols[side, :n] = own[:n] if side == 0 else own[n:]
        for q, ref in enumerate((t1, t2, t3) if side == 0 else (i1, i2, i3)):
            cols[side, (q + 1) * n : (q + 2) * n] = ref[...]
        s = dot_t(cols[side], rows[side]) * LOGIT_SCALE
        top = jnp.max(s, axis=0, keepdims=True)
        lse = top + jnp.log(jnp.sum(jnp.exp(s - top), axis=0, keepdims=True))
        part += [lse[:, q * n : (q + 1) * n] for q in range(SPANS)]
    for sigma in range(SPANS):
        v = jnp.concatenate([part[4 * (r // 4) + ((r % 4) ^ sigma)] for r in range(2 * SPANS)])
        to = pos ^ sigma

        def store(b, _):
            out[b * SPANS + to] = v
            return 0

        lax.fori_loop(0, count, store, 0)


def grad_kernel(count, *refs):
    got, own, core, x, t1, t2, t3, i1, i2, i3, tx1, tx2, tx3, ix1, ix2, ix3 = refs[:16]
    image_lse, text_lse, kept, sent, rows, cols = refs[16:]
    n = t1.shape[0]
    b = lax.axis_index("batch")

    def lse_of(block):
        at = lax.rem(block + count, count) * SPANS
        v = [got[at + s] for s in range(SPANS)]
        top = jnp.maximum(jnp.maximum(v[0], v[1]), jnp.maximum(v[2], v[3]))
        return top + jnp.log(sum(jnp.exp(a - top) for a in v))

    mine = lse_of(b)
    image_lse[...] = mine[0]
    text_lse[...] = mine[4]
    turned = mine.T
    for side in range(2):
        if side == 0:
            half = slice(n, 2 * n)
            pieces = [(own, x), (t1, tx1), (t2, tx2), (t3, tx3)]
        else:
            half = slice(0, n)
            pieces = [(own, x), (i1, ix1), (i2, ix2), (i3, ix3)]
        rows[side, :n] = own[half]
        rows[side, n:] = core[half]
        row_lse = jnp.concatenate([turned[:, 4 * side : 4 * side + 1], turned[:, 4 * side + 1 : 4 * side + 2]])
        total = jnp.zeros((2 * n, rows.shape[-1]), F32)
        for k, (near, far) in enumerate(pieces):
            if k == 0:
                other = slice(0, n) if side == 0 else slice(n, 2 * n)
                cols[side, k, :n] = near[other]
                cols[side, k, n:] = far[other]
                l = mine
            else:
                cols[side, k, :n] = near[...]
                cols[side, k, n:] = far[...]
                l = lse_of(b - k) if side == 0 else lse_of(b + k)
            at = 4 if side == 0 else 0
            col_lse = jnp.concatenate([l[at : at + 1], l[at + 2 : at + 3]], axis=1)
            c = cols[side, k]
            s = dot_t(rows[side], c) * LOGIT_SCALE
            w = 0.5 * jnp.exp(s - row_lse) + 0.5 * jnp.exp(s - col_lse)
            if k == 0:
                i = lax.broadcasted_iota(jnp.int32, s.shape, 0)
                j = lax.broadcasted_iota(jnp.int32, s.shape, 1)
                w = w - ((i == j) & (i < n)).astype(F32)
            total = total + jnp.dot(w.astype(BF16), c, preferred_element_type=F32)
        kept[side] = LOGIT_SCALE * total[:n]
        sent[side] = LOGIT_SCALE * total[n:]


def add_kernel(kept, got, image_grad, text_grad):
    image_grad[...] = kept[0] + got[0]
    text_grad[...] = kept[1] + got[1]


def body(image_embeds, text_embeds):
    n, width = image_embeds.shape
    count = lax.axis_size("batch")
    piece = jax.ShapeDtypeStruct((n, width), BF16)
    i0, t0, own = call(
        cast_kernel, (piece, piece, jax.ShapeDtypeStruct((2 * n, width), BF16)), [], 0, image_embeds, text_embeds
    )
    texts = [along(t0, k) for k in range(1, STEPS)]
    images = [along(i0, -k) for k in range(1, STEPS)]
    x = over_x(own)
    texts_x = [over_x(v) for v in texts]
    images_x = [over_x(v) for v in images]
    core = over_core(own)
    corex = over_core(x)
    send = call(
        functools.partial(stats_kernel, count),
        jax.ShapeDtypeStruct((count * SPANS, 2 * SPANS, n), F32),
        [pltpu.VMEM((2, SPANS * n, width), BF16), pltpu.VMEM((2, STEPS * n, width), BF16)],
        4 * SPANS * n * STEPS * n * width,
        own, core, x, corex, *texts, *images,
    )
    got = lax.all_to_all(send, AXES, 0, 0, tiled=True)
    row = jax.ShapeDtypeStruct((n,), F32)
    pair = jax.ShapeDtypeStruct((2, n, width), F32)
    image_lse, text_lse, kept, sent = call(
        functools.partial(grad_kernel, count),
        (row, row, pair, pair),
        [pltpu.VMEM((2, 2 * n, width), BF16), pltpu.VMEM((2, STEPS, 2 * n, width), BF16)],
        8 * 2 * n * STEPS * 2 * n * width,
        got, own, core, x, *texts, *images, *texts_x, *images_x,
    )
    grad = jax.ShapeDtypeStruct((n, width), F32)
    image_grad, text_grad = call(add_kernel, (grad, grad), [], 0, kept, over_core(sent))
    return (image_lse, text_lse, image_grad, text_grad)


def solution(mesh):
    in_specs = (P(("batch", "span"), None), P(("batch", "span"), None))
    out_specs = (
        P(("batch", "span")),
        P(("batch", "span")),
        P(("batch", "span"), None),
        P(("batch", "span"), None),
    )
    return jax.shard_map(body, mesh=mesh, in_specs=in_specs, out_specs=out_specs, check_vma=False)
```

```python
import functools

import jax
import jax.numpy as jnp
from jax import lax
from jax.experimental import pallas as pl
from jax.experimental.pallas import tpu as pltpu
from jax.sharding import PartitionSpec as P

STEPS = 4
LOGIT_SCALE = 5.0
AXES = ("batch", "span")
SPANS = 4
F32, BF16 = jnp.float32, jnp.bfloat16
VMEM_LIMIT = 32 * 1024 * 1024


def moved(value, target):
    count, spans = lax.axis_size("batch"), lax.axis_size("span")
    pairs = []
    for b in range(count):
        for s in range(spans):
            to_b, to_s = target(b, s)
            pairs.append((b * spans + s, (to_b % count) * spans + to_s))
    return lax.ppermute(value, AXES, pairs)


def over_core(value):
    return moved(value, lambda b, s: (b, s ^ 1))


def over_x(value):
    return moved(value, lambda b, s: (b, s ^ 2))


def along(value, steps):
    return moved(value, lambda b, s: (b + steps, s))


def in_pair(value):
    return moved(value, lambda b, s: (b ^ 1, s))


def across_pairs(value):
    return moved(value, lambda b, s: (b + (3 if b % 2 else -3), s))


def dot_t(a, b):
    return lax.dot_general(a, b, (((1,), (1,)), ((), ())), preferred_element_type=F32)


def call(kernel, out_shape, scratch, flops, *args, remote=()):
    whole = pl.BlockSpec(memory_space=pltpu.VMEM)
    size = sum(a.size * a.dtype.itemsize for a in args)
    return pl.pallas_call(
        kernel,
        out_shape=out_shape,
        in_specs=[pl.BlockSpec(memory_space=pl.ANY) if i in remote else whole for i in range(len(args))],
        out_specs=jax.tree.map(lambda _: whole, out_shape),
        scratch_shapes=scratch,
        compiler_params=pltpu.CompilerParams(vmem_limit_bytes=VMEM_LIMIT),
        cost_estimate=pl.CostEstimate(flops=flops, bytes_accessed=size, transcendentals=0),
    )(*args)


def cast_kernel(image, text, i_out, t_out, own, for_pair, for_across, i_in, t_in, sems):
    load_i = pltpu.make_async_copy(image, i_in, sems.at[0])
    load_t = pltpu.make_async_copy(text, t_in, sems.at[1])
    load_i.start()
    load_t.start()
    n = image.shape[0]
    odd = lax.rem(lax.axis_index("batch"), 2)
    load_i.wait()
    i = i_in[...].astype(BF16)
    i_out[...] = i
    own[n:] = i
    load_t.wait()
    t = t_in[...].astype(BF16)
    t_out[...] = t
    own[:n] = t

    @pl.when(odd == 0)
    def _():
        for_pair[...] = t
        for_across[...] = i

    @pl.when(odd == 1)
    def _():
        for_pair[...] = i
        for_across[...] = t


def fill_columns(cols, place, odd, own, a_t, a_i, b, pair, across):
    n = a_t.shape[0]
    at = slice(place * n, (place + 1) * n)
    cols[0, 0, at] = own[:n]
    cols[1, 0, at] = own[n:]
    cols[0, 1, at] = a_t[...]
    cols[1, 1, at] = a_i[...]
    cols[0, 2, at] = b[:n]
    cols[1, 2, at] = b[n:]
    cols[1 - odd, 3, at] = pair[...]
    cols[odd, 3, at] = across[...]


def stats_kernel(count, *refs):
    own, core, x, corex, a_t, a_i, b2, pair, across, out, rows, cols = refs
    n = a_t.shape[0]
    pos = lax.axis_index("span")
    odd = lax.rem(lax.axis_index("batch"), 2)
    fill_columns(cols, 0, odd, own, a_t, a_i, b2, pair, across)
    part = []
    for side in range(2):
        for q, ref in enumerate((own, core, x, corex)):
            rows[side, q * n : (q + 1) * n] = ref[n:] if side == 0 else ref[:n]
        s = dot_t(cols[side].reshape(STEPS * n, cols.shape[-1]), rows[side]) * LOGIT_SCALE
        top = jnp.max(s, axis=0, keepdims=True)
        lse = top + jnp.log(jnp.sum(jnp.exp(s - top), axis=0, keepdims=True))
        part += [lse[:, q * n : (q + 1) * n] for q in range(SPANS)]
    for sigma in range(SPANS):
        v = jnp.concatenate([part[4 * (r // 4) + ((r % 4) ^ sigma)] for r in range(2 * SPANS)])
        to = pos ^ sigma

        def store(b, _):
            out[b * SPANS + to] = v
            return 0

        lax.fori_loop(0, count, store, 0)


def grad_kernel(count, *refs):
    got, own, core, x, a_t, a_i, b2, pair, across, ax_t, ax_i, bx2, pairx, acrossx = refs[:14]
    image_lse, text_lse, kept, sent, rows, cols = refs[14:]
    n = a_t.shape[0]
    b = lax.axis_index("batch")
    odd = lax.rem(b, 2)

    def lse_of(block):
        at = lax.rem(block + count, count) * SPANS
        v = [got[at + s] for s in range(SPANS)]
        top = jnp.maximum(jnp.maximum(v[0], v[1]), jnp.maximum(v[2], v[3]))
        return top + jnp.log(sum(jnp.exp(a - top) for a in v))

    fill_columns(cols, 0, odd, own, a_t, a_i, b2, pair, across)
    fill_columns(cols, 1, odd, x, ax_t, ax_i, bx2, pairx, acrossx)
    mine = lse_of(b)
    image_lse[...] = mine[0]
    text_lse[...] = mine[4]
    turned = mine.T
    for side in range(2):
        half = slice(n, 2 * n) if side == 0 else slice(0, n)
        rows[side, :n] = own[half]
        rows[side, n:] = core[half]
        row_lse = jnp.concatenate([turned[:, 4 * side : 4 * side + 1], turned[:, 4 * side + 1 : 4 * side + 2]])
        total = jnp.zeros((2 * n, rows.shape[-1]), F32)
        steps = (0, -2, -1 - 2 * odd, -3 + 2 * odd) if side == 0 else (0, 2, 3 - 2 * odd, 1 + 2 * odd)
        for k, step in enumerate(steps):
            l = mine if k == 0 else lse_of(b + step)
            at = 4 if side == 0 else 0
            col_lse = jnp.concatenate([l[at : at + 1], l[at + 2 : at + 3]], axis=1)
            c = cols[side, k]
            s = dot_t(rows[side], c) * LOGIT_SCALE
            w = 0.5 * jnp.exp(s - row_lse) + 0.5 * jnp.exp(s - col_lse)
            if k == 0:
                i = lax.broadcasted_iota(jnp.int32, s.shape, 0)
                j = lax.broadcasted_iota(jnp.int32, s.shape, 1)
                w = w - ((i == j) & (i < n)).astype(F32)
            total = total + jnp.dot(w.astype(BF16), c, preferred_element_type=F32)
        kept[side] = LOGIT_SCALE * total[:n]
        sent[side] = LOGIT_SCALE * total[n:]


def add_kernel(kept, got, image_grad, text_grad):
    image_grad[...] = kept[0] + got[0]
    text_grad[...] = kept[1] + got[1]


def body(image_embeds, text_embeds):
    n, width = image_embeds.shape
    count = lax.axis_size("batch")
    assert count % 2 == 0
    piece = jax.ShapeDtypeStruct((n, width), BF16)
    i0, t0, own, for_pair, for_across = call(
        cast_kernel,
        (piece, piece, jax.ShapeDtypeStruct((2 * n, width), BF16), piece, piece),
        [pltpu.VMEM((n, width), F32), pltpu.VMEM((n, width), F32), pltpu.SemaphoreType.DMA((2,))],
        0, image_embeds, text_embeds, remote=(0, 1),
    )
    a_t, a_i = along(t0, 2), along(i0, -2)
    pair, across = in_pair(for_pair), across_pairs(for_across)
    b2 = in_pair(jnp.concatenate([a_t, a_i]))
    x = over_x(own)
    far = [over_x(v) for v in (a_t, a_i, b2, pair, across)]
    core = over_core(own)
    corex = over_core(x)
    send = call(
        functools.partial(stats_kernel, count),
        jax.ShapeDtypeStruct((count * SPANS, 2 * SPANS, n), F32),
        [pltpu.VMEM((2, SPANS * n, width), BF16), pltpu.VMEM((2, STEPS, n, width), BF16)],
        4 * SPANS * n * STEPS * n * width,
        own, core, x, corex, a_t, a_i, b2, pair, across,
    )
    got = lax.all_to_all(send, AXES, 0, 0, tiled=True)
    row = jax.ShapeDtypeStruct((n,), F32)
    both = jax.ShapeDtypeStruct((2, n, width), F32)
    image_lse, text_lse, kept, sent = call(
        functools.partial(grad_kernel, count),
        (row, row, both, both),
        [pltpu.VMEM((2, 2 * n, width), BF16), pltpu.VMEM((2, STEPS, 2 * n, width), BF16)],
        8 * 2 * n * STEPS * 2 * n * width,
        got, own, core, x, a_t, a_i, b2, pair, across, *far,
    )
    grad = jax.ShapeDtypeStruct((n, width), F32)
    image_grad, text_grad = call(add_kernel, (grad, grad), [], 0, kept, over_core(sent))
    return (image_lse, text_lse, image_grad, text_grad)


def solution(mesh):
    in_specs = (P(("batch", "span"), None), P(("batch", "span"), None))
    out_specs = (
        P(("batch", "span")),
        P(("batch", "span")),
        P(("batch", "span"), None),
        P(("batch", "span"), None),
    )
    return jax.shard_map(body, mesh=mesh, in_specs=in_specs, out_specs=out_specs, check_vma=False)
```

```python
import functools

import jax
import jax.numpy as jnp
from jax import lax
from jax.experimental import pallas as pl
from jax.experimental.pallas import tpu as pltpu
from jax.sharding import PartitionSpec as P

STEPS = 4
LOGIT_SCALE = 5.0
AXES = ("batch", "span")
SPANS = 4
F32, BF16 = jnp.float32, jnp.bfloat16
VMEM_LIMIT = 16 * 1024 * 1024


def moved(value, target):
    count, spans = lax.axis_size("batch"), lax.axis_size("span")
    pairs = []
    for b in range(count):
        for s in range(spans):
            to_b, to_s = target(b, s)
            pairs.append((b * spans + s, (to_b % count) * spans + to_s))
    return lax.ppermute(value, AXES, pairs)


def over_core(value):
    return moved(value, lambda b, s: (b, s ^ 1))


def over_x(value):
    return moved(value, lambda b, s: (b, s ^ 2))


def along(value, steps):
    return moved(value, lambda b, s: (b + steps, s))


def in_pair(value):
    return moved(value, lambda b, s: (b ^ 1, s))


def across_pairs(value):
    return moved(value, lambda b, s: (b + (3 if b % 2 else -3), s))


def after(value, first):
    return lax.optimization_barrier((value, first))[0]


def dot_t(a, b):
    return lax.dot_general(a, b, (((1,), (1,)), ((), ())), preferred_element_type=F32)


def call(kernel, out_shape, scratch, flops, *args, remote=()):
    whole = pl.BlockSpec(memory_space=pltpu.VMEM)
    size = sum(a.size * a.dtype.itemsize for a in args)
    return pl.pallas_call(
        kernel,
        out_shape=out_shape,
        in_specs=[pl.BlockSpec(memory_space=pltpu.HBM) if i in remote else whole for i in range(len(args))],
        out_specs=jax.tree.map(lambda _: whole, out_shape),
        scratch_shapes=scratch,
        compiler_params=pltpu.CompilerParams(vmem_limit_bytes=VMEM_LIMIT),
        cost_estimate=pl.CostEstimate(flops=flops, bytes_accessed=size, transcendentals=0),
    )(*args)


def pack_kernel(image, text, own, for_pair, for_across):
    n = image.shape[0]
    odd = lax.rem(lax.axis_index("batch"), 2)
    own[:n] = text[...]
    own[n:] = image[...]

    @pl.when(odd == 0)
    def _():
        for_pair[...] = text[...]
        for_across[...] = image[...]

    @pl.when(odd == 1)
    def _():
        for_pair[...] = image[...]
        for_across[...] = text[...]


def fill_columns(cols, place, odd, own, ab, b, pc):
    n = own.shape[0] // 2
    at = slice(place * n, (place + 1) * n)
    for side in range(2):
        for slot, ref in enumerate((own, ab, b)):
            cols[side, slot, at] = ref[side * n : (side + 1) * n]
    cols[1 - odd, 3, at] = pc[:n]
    cols[odd, 3, at] = pc[n:]


def stats_kernel(count, *refs):
    own, core, x, corex, ab, b2, pc, out, rows, cols = refs
    n = own.shape[0] // 2
    pos = lax.axis_index("span")
    odd = lax.rem(lax.axis_index("batch"), 2)
    fill_columns(cols, 0, odd, own, ab, b2, pc)
    part = []
    for side in range(2):
        for q, ref in enumerate((own, core, x, corex)):
            rows[side, q * n : (q + 1) * n] = ref[n:] if side == 0 else ref[:n]
        s = dot_t(cols[side].reshape(STEPS * n, cols.shape[-1]), rows[side]) * LOGIT_SCALE
        top = jnp.max(s, axis=0, keepdims=True)
        lse = top + jnp.log(jnp.sum(jnp.exp(s - top), axis=0, keepdims=True))
        part += [lse[:, q * n : (q + 1) * n] for q in range(SPANS)]
    for sigma in range(SPANS):
        v = jnp.concatenate([part[4 * (r // 4) + ((r % 4) ^ sigma)] for r in range(2 * SPANS)])
        to = pos ^ sigma

        def store(b, _):
            out[b * SPANS + to] = v
            return 0

        lax.fori_loop(0, count, store, 0)


def grad_kernel(count, *refs):
    got, own, core, x, ab, b2, pc, abx, bx2, pcx = refs[:10]
    image_lse, text_lse, kept, sent, got_in, rows, cols, sem = refs[10:]
    load = pltpu.make_async_copy(got, got_in, sem)
    load.start()
    n = own.shape[0] // 2
    b = lax.axis_index("batch")
    odd = lax.rem(b, 2)

    def lse_of(block):
        at = lax.rem(block + count, count) * SPANS
        v = [got_in[at + s] for s in range(SPANS)]
        top = jnp.maximum(jnp.maximum(v[0], v[1]), jnp.maximum(v[2], v[3]))
        return top + jnp.log(sum(jnp.exp(a - top) for a in v))

    fill_columns(cols, 0, odd, own, ab, b2, pc)
    fill_columns(cols, 1, odd, x, abx, bx2, pcx)
    load.wait()
    mine = lse_of(b)
    image_lse[...] = mine[0]
    text_lse[...] = mine[4]
    turned = mine.T
    for side in range(2):
        half = slice(n, 2 * n) if side == 0 else slice(0, n)
        rows[side, :n] = own[half]
        rows[side, n:] = core[half]
        row_lse = jnp.concatenate([turned[:, 4 * side : 4 * side + 1], turned[:, 4 * side + 1 : 4 * side + 2]])
        total = jnp.zeros((2 * n, rows.shape[-1]), F32)
        steps = (0, -2, -1 - 2 * odd, -3 + 2 * odd) if side == 0 else (0, 2, 3 - 2 * odd, 1 + 2 * odd)
        for k, step in enumerate(steps):
            l = mine if k == 0 else lse_of(b + step)
            at = 4 if side == 0 else 0
            col_lse = jnp.concatenate([l[at : at + 1], l[at + 2 : at + 3]], axis=1)
            c = cols[side, k]
            s = dot_t(rows[side], c) * LOGIT_SCALE
            w = 0.5 * jnp.exp(s - row_lse) + 0.5 * jnp.exp(s - col_lse)
            if k == 0:
                i = lax.broadcasted_iota(jnp.int32, s.shape, 0)
                j = lax.broadcasted_iota(jnp.int32, s.shape, 1)
                w = w - ((i == j) & (i < n)).astype(F32)
            total = total + jnp.dot(w.astype(BF16), c, preferred_element_type=F32)
        kept[side] = LOGIT_SCALE * total[:n]
        sent[side] = LOGIT_SCALE * total[n:]


def add_kernel(kept, got, image_grad, text_grad):
    image_grad[...] = kept[0] + got[0]
    text_grad[...] = kept[1] + got[1]


def body(image_embeds, text_embeds):
    n, width = image_embeds.shape
    count = lax.axis_size("batch")
    assert count % 2 == 0
    piece = jax.ShapeDtypeStruct((n, width), BF16)
    i0, t0 = image_embeds.astype(BF16), text_embeds.astype(BF16)
    own, for_pair, for_across = call(
        pack_kernel, (jax.ShapeDtypeStruct((2 * n, width), BF16), piece, piece), [], 0, i0, t0
    )
    a_t, a_i = along(t0, 2), along(i0, -2)
    pair, across = in_pair(for_pair), across_pairs(for_across)
    ab, pc = jnp.concatenate([a_t, a_i]), jnp.concatenate([pair, across])
    b2 = in_pair(ab)
    core = over_core(own)
    x = over_x(own)
    corex = over_core(x)
    far_ab, far_b, far_pc = [over_x(v) for v in (ab, b2, pc)]
    far_ab, core, _ = lax.optimization_barrier((far_ab, core, over_core(pc)))
    send = call(
        functools.partial(stats_kernel, count),
        jax.ShapeDtypeStruct((count * SPANS, 2 * SPANS, n), F32),
        [pltpu.VMEM((2, SPANS * n, width), BF16), pltpu.VMEM((2, STEPS, n, width), BF16)],
        4 * SPANS * n * STEPS * n * width,
        own, core, x, corex, ab, b2, pc,
    )
    far_pc, send = lax.optimization_barrier((far_pc, send))
    got = lax.all_to_all(send, AXES, 0, 0, tiled=True)
    row = jax.ShapeDtypeStruct((n,), F32)
    both = jax.ShapeDtypeStruct((2, n, width), F32)
    image_lse, text_lse, kept, sent = call(
        functools.partial(grad_kernel, count),
        (row, row, both, both),
        [
            pltpu.VMEM(got.shape, F32),
            pltpu.VMEM((2, 2 * n, width), BF16),
            pltpu.VMEM((2, STEPS, 2 * n, width), BF16),
            pltpu.SemaphoreType.DMA,
        ],
        8 * 2 * n * STEPS * 2 * n * width,
        got, own, core, x, ab, b2, pc, far_ab, far_b, far_pc, remote=(0,),
    )
    grad = jax.ShapeDtypeStruct((n, width), F32)
    image_grad, text_grad = call(add_kernel, (grad, grad), [], 0, kept, over_core(sent))
    return (image_lse, text_lse, image_grad, text_grad)


def solution(mesh):
    in_specs = (P(("batch", "span"), None), P(("batch", "span"), None))
    out_specs = (
        P(("batch", "span")),
        P(("batch", "span")),
        P(("batch", "span"), None),
        P(("batch", "span"), None),
    )
    return jax.shard_map(body, mesh=mesh, in_specs=in_specs, out_specs=out_specs, check_vma=False)
```

```python
import functools

import jax
import jax.numpy as jnp
from jax import lax
from jax.experimental import pallas as pl
from jax.experimental.pallas import tpu as pltpu
from jax.sharding import PartitionSpec as P

STEPS = 4
LOGIT_SCALE = 5.0
AXES = ("batch", "span")
SPANS = 4
F32, BF16 = jnp.float32, jnp.bfloat16
VMEM_LIMIT = 16 * 1024 * 1024


def moved(value, target):
    count, spans = lax.axis_size("batch"), lax.axis_size("span")
    pairs = []
    for b in range(count):
        for s in range(spans):
            to_b, to_s = target(b, s)
            pairs.append((b * spans + s, (to_b % count) * spans + to_s))
    return lax.ppermute(value, AXES, pairs)


def over_core(value):
    return moved(value, lambda b, s: (b, s ^ 1))


def over_x(value):
    return moved(value, lambda b, s: (b, s ^ 2))


def along(value, steps):
    return moved(value, lambda b, s: (b + steps, s))


def in_pair(value):
    return moved(value, lambda b, s: (b ^ 1, s))


def across_pairs(value):
    return moved(value, lambda b, s: (b + (3 if b % 2 else -3), s))


def after(value, first):
    return lax.optimization_barrier((value, first))[0]


def dot_t(a, b):
    return lax.dot_general(a, b, (((1,), (1,)), ((), ())), preferred_element_type=F32)


def call(kernel, out_shape, scratch, flops, *args, remote=()):
    whole = pl.BlockSpec(memory_space=pltpu.VMEM)
    size = sum(a.size * a.dtype.itemsize for a in args)
    return pl.pallas_call(
        kernel,
        out_shape=out_shape,
        in_specs=[pl.BlockSpec(memory_space=pltpu.HBM) if i in remote else whole for i in range(len(args))],
        out_specs=jax.tree.map(lambda _: whole, out_shape),
        scratch_shapes=scratch,
        compiler_params=pltpu.CompilerParams(vmem_limit_bytes=VMEM_LIMIT),
        cost_estimate=pl.CostEstimate(flops=flops, bytes_accessed=size, transcendentals=0),
    )(*args)


def pack_kernel(image, text, own, for_pair, for_across):
    n = image.shape[0]
    odd = lax.rem(lax.axis_index("batch"), 2)
    own[:n] = text[...]
    own[n:] = image[...]

    @pl.when(odd == 0)
    def _():
        for_pair[...] = text[...]
        for_across[...] = image[...]

    @pl.when(odd == 1)
    def _():
        for_pair[...] = image[...]
        for_across[...] = text[...]


def fill_columns(cols, place, odd, own, ab, b, pc):
    n = own.shape[0] // 2
    at = slice(place * n, (place + 1) * n)
    for side in range(2):
        for slot, ref in enumerate((own, ab, b)):
            cols[side, slot, at] = ref[side * n : (side + 1) * n]
    cols[1 - odd, 3, at] = pc[:n]
    cols[odd, 3, at] = pc[n:]


def stats_kernel(count, *refs):
    own, core, x, corex, ab, b2, pc, out, rows, cols = refs
    n = own.shape[0] // 2
    pos = lax.axis_index("span")
    odd = lax.rem(lax.axis_index("batch"), 2)
    fill_columns(cols, 0, odd, own, ab, b2, pc)
    part = []
    for side in range(2):
        for q, ref in enumerate((own, core, x, corex)):
            rows[side, q * n : (q + 1) * n] = ref[n:] if side == 0 else ref[:n]
        s = dot_t(cols[side].reshape(STEPS * n, cols.shape[-1]), rows[side]) * LOGIT_SCALE
        top = jnp.max(s, axis=0, keepdims=True)
        lse = top + jnp.log(jnp.sum(jnp.exp(s - top), axis=0, keepdims=True))
        part += [lse[:, q * n : (q + 1) * n] for q in range(SPANS)]
    for sigma in range(SPANS):
        v = jnp.concatenate([part[4 * (r // 4) + ((r % 4) ^ sigma)] for r in range(2 * SPANS)])
        to = pos ^ sigma

        def store(b, _):
            out[b * SPANS + to] = v
            return 0

        lax.fori_loop(0, count, store, 0)


def grad_kernel(count, *refs):
    got, own, core, x, ab, b2, pc, abx, bx2, pcx = refs[:10]
    image_lse, text_lse, kept, sent, got_in, rows, cols, sem = refs[10:]
    load = pltpu.make_async_copy(got, got_in, sem)
    load.start()
    n = own.shape[0] // 2
    b = lax.axis_index("batch")
    odd = lax.rem(b, 2)

    def lse_of(block):
        at = lax.rem(block + count, count) * SPANS
        v = [got_in[at + s] for s in range(SPANS)]
        top = jnp.maximum(jnp.maximum(v[0], v[1]), jnp.maximum(v[2], v[3]))
        return top + jnp.log(sum(jnp.exp(a - top) for a in v))

    fill_columns(cols, 0, odd, own, ab, b2, pc)
    fill_columns(cols, 1, odd, x, abx, bx2, pcx)
    load.wait()
    mine = lse_of(b)
    image_lse[...] = mine[0]
    text_lse[...] = mine[4]
    turned = mine.T
    for side in range(2):
        half = slice(n, 2 * n) if side == 0 else slice(0, n)
        rows[side, :n] = own[half]
        rows[side, n:] = core[half]
        row_lse = jnp.concatenate([turned[:, 4 * side : 4 * side + 1], turned[:, 4 * side + 1 : 4 * side + 2]])
        total = jnp.zeros((2 * n, rows.shape[-1]), F32)
        steps = (0, -2, -1 - 2 * odd, -3 + 2 * odd) if side == 0 else (0, 2, 3 - 2 * odd, 1 + 2 * odd)
        for k, step in enumerate(steps):
            l = mine if k == 0 else lse_of(b + step)
            at = 4 if side == 0 else 0
            col_lse = jnp.concatenate([l[at : at + 1], l[at + 2 : at + 3]], axis=1)
            c = cols[side, k]
            s = dot_t(rows[side], c) * LOGIT_SCALE
            w = 0.5 * jnp.exp(s - row_lse) + 0.5 * jnp.exp(s - col_lse)
            if k == 0:
                i = lax.broadcasted_iota(jnp.int32, s.shape, 0)
                j = lax.broadcasted_iota(jnp.int32, s.shape, 1)
                w = w - ((i == j) & (i < n)).astype(F32)
            total = total + jnp.dot(w.astype(BF16), c, preferred_element_type=F32)
        kept[side] = LOGIT_SCALE * total[:n]
        sent[side] = LOGIT_SCALE * total[n:]


def add_kernel(kept, got, image_grad, text_grad):
    image_grad[...] = kept[0] + got[0]
    text_grad[...] = kept[1] + got[1]


def body(image_embeds, text_embeds):
    n, width = image_embeds.shape
    count = lax.axis_size("batch")
    assert count % 2 == 0
    piece = jax.ShapeDtypeStruct((n, width), BF16)
    i0, t0 = image_embeds.astype(BF16), text_embeds.astype(BF16)
    own, for_pair, for_across = call(
        pack_kernel, (jax.ShapeDtypeStruct((2 * n, width), BF16), piece, piece), [], 0, i0, t0
    )
    a_t, a_i = along(t0, 2), along(i0, -2)
    pair, across = in_pair(for_pair), across_pairs(for_across)
    ab, pc = jnp.concatenate([a_t, a_i]), jnp.concatenate([pair, across])
    b2 = in_pair(ab)
    core = over_core(own)
    x = over_x(own)
    corex = over_core(x)
    far_ab, far_pc = over_x(ab), over_x(pc)
    far_b = in_pair(far_ab)
    far_ab, core, _ = lax.optimization_barrier((far_ab, core, over_core(pc)))
    send = call(
        functools.partial(stats_kernel, count),
        jax.ShapeDtypeStruct((count * SPANS, 2 * SPANS, n), F32),
        [pltpu.VMEM((2, SPANS * n, width), BF16), pltpu.VMEM((2, STEPS, n, width), BF16)],
        4 * SPANS * n * STEPS * n * width,
        own, core, x, corex, ab, b2, pc,
    )
    far_pc, send = lax.optimization_barrier((far_pc, send))
    got = lax.all_to_all(send, AXES, 0, 0, tiled=True)
    row = jax.ShapeDtypeStruct((n,), F32)
    both = jax.ShapeDtypeStruct((2, n, width), F32)
    image_lse, text_lse, kept, sent = call(
        functools.partial(grad_kernel, count),
        (row, row, both, both),
        [
            pltpu.VMEM(got.shape, F32),
            pltpu.VMEM((2, 2 * n, width), BF16),
            pltpu.VMEM((2, STEPS, 2 * n, width), BF16),
            pltpu.SemaphoreType.DMA,
        ],
        8 * 2 * n * STEPS * 2 * n * width,
        got, own, core, x, ab, b2, pc, far_ab, far_b, far_pc, remote=(0,),
    )
    grad = jax.ShapeDtypeStruct((n, width), F32)
    image_grad, text_grad = call(add_kernel, (grad, grad), [], 0, kept, over_core(sent))
    return (image_lse, text_lse, image_grad, text_grad)


def solution(mesh):
    in_specs = (P(("batch", "span"), None), P(("batch", "span"), None))
    out_specs = (
        P(("batch", "span")),
        P(("batch", "span")),
        P(("batch", "span"), None),
        P(("batch", "span"), None),
    )
    return jax.shard_map(body, mesh=mesh, in_specs=in_specs, out_specs=out_specs, check_vma=False)
```

```python
import functools

import jax
import jax.numpy as jnp
from jax import lax
from jax.experimental import pallas as pl
from jax.experimental.pallas import tpu as pltpu
from jax.sharding import PartitionSpec as P

STEPS = 4
LOGIT_SCALE = 5.0
AXES = ("batch", "span")
SPANS = 4
F32, BF16 = jnp.float32, jnp.bfloat16
VMEM_LIMIT = 16 * 1024 * 1024


def moved(value, target):
    count, spans = lax.axis_size("batch"), lax.axis_size("span")
    pairs = []
    for b in range(count):
        for s in range(spans):
            to_b, to_s = target(b, s)
            pairs.append((b * spans + s, (to_b % count) * spans + to_s))
    return lax.ppermute(value, AXES, pairs)


def over_core(value):
    return moved(value, lambda b, s: (b, s ^ 1))


def over_x(value):
    return moved(value, lambda b, s: (b, s ^ 2))


def along(value, steps):
    return moved(value, lambda b, s: (b + steps, s))


def in_pair(value):
    return moved(value, lambda b, s: (b ^ 1, s))


def across_pairs(value):
    return moved(value, lambda b, s: (b + (3 if b % 2 else -3), s))


def after(value, first):
    return lax.optimization_barrier((value, first))[0]


def dot_t(a, b):
    return lax.dot_general(a, b, (((1,), (1,)), ((), ())), preferred_element_type=F32)


def call(kernel, out_shape, scratch, flops, *args, remote=()):
    whole = pl.BlockSpec(memory_space=pltpu.VMEM)
    size = sum(a.size * a.dtype.itemsize for a in args)
    return pl.pallas_call(
        kernel,
        out_shape=out_shape,
        in_specs=[pl.BlockSpec(memory_space=pl.ANY) if i in remote else whole for i in range(len(args))],
        out_specs=jax.tree.map(lambda _: whole, out_shape),
        scratch_shapes=scratch,
        compiler_params=pltpu.CompilerParams(vmem_limit_bytes=VMEM_LIMIT),
        cost_estimate=pl.CostEstimate(flops=flops, bytes_accessed=size, transcendentals=0),
    )(*args)


def pack_kernel(image, text, own, for_pair, for_across):
    n = image.shape[0]
    odd = lax.rem(lax.axis_index("batch"), 2)
    own[:n] = text[...]
    own[n:] = image[...]

    @pl.when(odd == 0)
    def _():
        for_pair[...] = text[...]
        for_across[...] = image[...]

    @pl.when(odd == 1)
    def _():
        for_pair[...] = image[...]
        for_across[...] = text[...]


def fill_columns(cols, place, odd, own, ab, b, pc):
    n = own.shape[0] // 2
    at = slice(place * n, (place + 1) * n)
    for side in range(2):
        for slot, ref in enumerate((own, ab, b)):
            if ref is not None:
                cols[side, slot, at] = ref[side * n : (side + 1) * n]
    cols[1 - odd, 3, at] = pc[:n]
    cols[odd, 3, at] = pc[n:]


def stats_kernel(count, *refs):
    own, core, x, corex, ab, b2, pc, out, rows, cols = refs
    n = own.shape[0] // 2
    pos = lax.axis_index("span")
    odd = lax.rem(lax.axis_index("batch"), 2)
    fill_columns(cols, 0, odd, own, ab, b2, pc)
    part = []
    for side in range(2):
        for q, ref in enumerate((own, core, x, corex)):
            rows[side, q * n : (q + 1) * n] = ref[n:] if side == 0 else ref[:n]
        s = dot_t(cols[side].reshape(STEPS * n, cols.shape[-1]), rows[side]) * LOGIT_SCALE
        top = jnp.max(s, axis=0, keepdims=True)
        lse = top + jnp.log(jnp.sum(jnp.exp(s - top), axis=0, keepdims=True))
        part += [lse[:, q * n : (q + 1) * n] for q in range(SPANS)]
    for sigma in range(SPANS):
        v = jnp.concatenate([part[4 * (r // 4) + ((r % 4) ^ sigma)] for r in range(2 * SPANS)])
        to = pos ^ sigma

        def store(b, _):
            out[b * SPANS + to] = v
            return 0

        lax.fori_loop(0, count, store, 0)


def grad_kernel(count, *refs):
    got, own, core, x, ab, b2, pc, abx, bx2, pcx = refs[:10]
    image_lse, text_lse, kept, sent, rows, cols, weights, sems = refs[10:]
    n = own.shape[0] // 2
    b = lax.axis_index("batch")
    odd = lax.rem(b, 2)
    loads = [
        pltpu.make_async_copy(bx2.at[pl.ds(side * n, n)], cols.at[side, 2, pl.ds(n, n)], sems.at[side])
        for side in range(2)
    ]
    for load in loads:
        load.start()

    def lse_of(block):
        at = lax.rem(block + count, count) * SPANS
        v = [got[at + s] for s in range(SPANS)]
        top = jnp.maximum(jnp.maximum(v[0], v[1]), jnp.maximum(v[2], v[3]))
        return top + jnp.log(sum(jnp.exp(a - top) for a in v))

    fill_columns(cols, 0, odd, own, ab, b2, pc)
    fill_columns(cols, 1, odd, x, abx, None, pcx)
    mine = lse_of(b)
    image_lse[...] = mine[0]
    text_lse[...] = mine[SPANS]
    turned = mine.T
    for side in range(2):
        half = slice(n, 2 * n) if side == 0 else slice(0, n)
        rows[side, :n] = own[half]
        rows[side, n:] = core[half]
        at = SPANS * side
        row_lse = jnp.concatenate([turned[:, at : at + 1], turned[:, at + 1 : at + 2]])
        steps = (0, -2, -1 - 2 * odd, -3 + 2 * odd) if side == 0 else (0, 2, 3 - 2 * odd, 1 + 2 * odd)
        at = SPANS * (1 - side)
        for k in (0, 1, 3, 2):
            if k == 2:
                loads[side].wait()
            l = mine if k == 0 else lse_of(b + steps[k])
            col_lse = jnp.concatenate([l[at : at + 1], l[at + 2 : at + 3]], axis=1)
            s = dot_t(rows[side], cols[side, k]) * LOGIT_SCALE
            w = 0.5 * (jnp.exp(s - row_lse) + jnp.exp(s - col_lse))
            if k == 0:
                i = lax.broadcasted_iota(jnp.int32, s.shape, 0)
                j = lax.broadcasted_iota(jnp.int32, s.shape, 1)
                w = w - ((i == j) & (i < n)).astype(F32)
            weights[side, :, k * 2 * n : (k + 1) * 2 * n] = w.astype(BF16)
        total = LOGIT_SCALE * jnp.dot(
            weights[side], cols[side].reshape(STEPS * 2 * n, cols.shape[-1]), preferred_element_type=F32
        )
        kept[side] = total[:n]
        sent[side] = total[n:]


def add_kernel(kept, got, image_grad, text_grad):
    image_grad[...] = kept[0] + got[0]
    text_grad[...] = kept[1] + got[1]


def body(image_embeds, text_embeds):
    n, width = image_embeds.shape
    count = lax.axis_size("batch")
    assert count % 2 == 0
    piece = jax.ShapeDtypeStruct((n, width), BF16)
    i0, t0 = image_embeds.astype(BF16), text_embeds.astype(BF16)
    own, for_pair, for_across = call(
        pack_kernel, (jax.ShapeDtypeStruct((2 * n, width), BF16), piece, piece), [], 0, i0, t0
    )
    a_t, a_i = along(t0, 2), along(i0, -2)
    pair, across = in_pair(for_pair), across_pairs(for_across)
    ab, pc = jnp.concatenate([a_t, a_i]), jnp.concatenate([pair, across])
    b2 = in_pair(ab)
    core = over_core(own)
    x = over_x(own)
    corex = over_core(x)
    far_ab, far_pc = over_x(ab), over_x(pc)
    far_b = in_pair(far_ab)
    far_ab, core, _ = lax.optimization_barrier((far_ab, core, over_core(pc)))
    send = call(
        functools.partial(stats_kernel, count),
        jax.ShapeDtypeStruct((count * SPANS, 2 * SPANS, n), F32),
        [pltpu.VMEM((2, SPANS * n, width), BF16), pltpu.VMEM((2, STEPS, n, width), BF16)],
        4 * SPANS * n * STEPS * n * width,
        own, core, x, corex, ab, b2, pc,
    )
    far_pc, send = lax.optimization_barrier((far_pc, send))
    got = lax.all_to_all(send, AXES, 0, 0, tiled=True)
    row = jax.ShapeDtypeStruct((n,), F32)
    both = jax.ShapeDtypeStruct((2, n, width), F32)
    image_lse, text_lse, kept, sent = call(
        functools.partial(grad_kernel, count),
        (row, row, both, both),
        [
            pltpu.VMEM((2, 2 * n, width), BF16),
            pltpu.VMEM((2, STEPS, 2 * n, width), BF16),
            pltpu.VMEM((2, 2 * n, STEPS * 2 * n), BF16),
            pltpu.SemaphoreType.DMA((2,)),
        ],
        8 * 2 * n * STEPS * 2 * n * width,
        got, own, core, x, ab, b2, pc, far_ab, far_b, far_pc, remote=(8,),
    )
    grad = jax.ShapeDtypeStruct((n, width), F32)
    image_grad, text_grad = call(add_kernel, (grad, grad), [], 0, kept, over_core(sent))
    return (image_lse, text_lse, image_grad, text_grad)


def solution(mesh):
    in_specs = (P(("batch", "span"), None), P(("batch", "span"), None))
    out_specs = (
        P(("batch", "span")),
        P(("batch", "span")),
        P(("batch", "span"), None),
        P(("batch", "span"), None),
    )
    return jax.shard_map(body, mesh=mesh, in_specs=in_specs, out_specs=out_specs, check_vma=False)
```

```python
import functools

import jax
import jax.numpy as jnp
from jax import lax
from jax.experimental import pallas as pl
from jax.experimental.pallas import tpu as pltpu
from jax.sharding import PartitionSpec as P

STEPS = 4
LOGIT_SCALE = 5.0
AXES = ("batch", "span")
SPANS = 4
F32, BF16 = jnp.float32, jnp.bfloat16
VMEM_LIMIT = 16 * 1024 * 1024


def moved(value, target):
    count, spans = lax.axis_size("batch"), lax.axis_size("span")
    pairs = []
    for b in range(count):
        for s in range(spans):
            to_b, to_s = target(b, s)
            pairs.append((b * spans + s, (to_b % count) * spans + to_s))
    return lax.ppermute(value, AXES, pairs)


def over_core(value):
    return moved(value, lambda b, s: (b, s ^ 1))


def over_x(value):
    return moved(value, lambda b, s: (b, s ^ 2))


def along(value, steps):
    return moved(value, lambda b, s: (b + steps, s))


def in_pair(value):
    return moved(value, lambda b, s: (b ^ 1, s))


def across_pairs(value):
    return moved(value, lambda b, s: (b + (3 if b % 2 else -3), s))


def after(value, first):
    return lax.optimization_barrier((value, first))[0]


def dot_t(a, b):
    return lax.dot_general(a, b, (((1,), (1,)), ((), ())), preferred_element_type=F32)


def call(kernel, out_shape, scratch, flops, *args, remote=()):
    whole = pl.BlockSpec(memory_space=pltpu.VMEM)
    size = sum(a.size * a.dtype.itemsize for a in args)
    return pl.pallas_call(
        kernel,
        out_shape=out_shape,
        in_specs=[pl.BlockSpec(memory_space=pl.ANY) if i in remote else whole for i in range(len(args))],
        out_specs=jax.tree.map(lambda _: whole, out_shape),
        scratch_shapes=scratch,
        compiler_params=pltpu.CompilerParams(vmem_limit_bytes=VMEM_LIMIT),
        cost_estimate=pl.CostEstimate(flops=flops, bytes_accessed=size, transcendentals=0),
    )(*args)


def pack_kernel(image, text, own, for_pair, for_across):
    n = image.shape[0]
    odd = lax.rem(lax.axis_index("batch"), 2)
    own[:n] = text[...]
    own[n:] = image[...]

    @pl.when(odd == 0)
    def _():
        for_pair[...] = text[...]
        for_across[...] = image[...]

    @pl.when(odd == 1)
    def _():
        for_pair[...] = image[...]
        for_across[...] = text[...]


def fill_columns(cols, place, odd, own, ab, b, pc):
    n = own.shape[0] // 2
    at = slice(place * n, (place + 1) * n)
    for side in range(2):
        for slot, ref in enumerate((own, ab, b)):
            if ref is not None:
                cols[side, slot, at] = ref[side * n : (side + 1) * n]
    cols[1 - odd, 3, at] = pc[:n]
    cols[odd, 3, at] = pc[n:]


def stats_kernel(own, core, x, corex, ab, pc, part, rows, cols):
    n = own.shape[0] // 2
    odd = lax.rem(lax.axis_index("batch"), 2)
    for side in range(2):
        for q, ref in enumerate((own, core, x, corex)):
            rows[side, q * n : (q + 1) * n] = ref[n:] if side == 0 else ref[:n]
        for slot, ref in enumerate((own, ab)):
            cols[side, slot] = ref[side * n : (side + 1) * n]
    cols[1 - odd, 2] = pc[:n]
    cols[odd, 2] = pc[n:]
    for side in range(2):
        s = dot_t(cols[side].reshape((STEPS - 1) * n, cols.shape[-1]), rows[side]) * LOGIT_SCALE
        top = jnp.max(s, axis=0, keepdims=True)
        part[side] = (top + jnp.log(jnp.sum(jnp.exp(s - top), axis=0, keepdims=True)))[0]


def finish_kernel(count, part, own, core, x, corex, b2, _, out, rows):
    n = own.shape[0] // 2
    pos = lax.axis_index("span")
    done = []
    for side in range(2):
        for q, ref in enumerate((own, core, x, corex)):
            rows[side, q * n : (q + 1) * n] = ref[n:] if side == 0 else ref[:n]
        s = dot_t(b2[side * n : (side + 1) * n], rows[side]) * LOGIT_SCALE
        before = part[side : side + 1]
        top = jnp.maximum(before, jnp.max(s, axis=0, keepdims=True))
        lse = top + jnp.log(jnp.exp(before - top) + jnp.sum(jnp.exp(s - top), axis=0, keepdims=True))
        done += [lse[:, q * n : (q + 1) * n] for q in range(SPANS)]
    for sigma in range(SPANS):
        v = jnp.concatenate([done[4 * (r // 4) + ((r % 4) ^ sigma)] for r in range(2 * SPANS)])
        to = pos ^ sigma

        def store(b, _):
            out[b * SPANS + to] = v
            return 0

        lax.fori_loop(0, count, store, 0)


def grad_kernel(count, *refs):
    got, own, core, x, ab, b2, pc, abx, bx2, pcx = refs[:10]
    image_lse, text_lse, kept, sent, rows, cols, weights, sems = refs[10:]
    n = own.shape[0] // 2
    b = lax.axis_index("batch")
    odd = lax.rem(b, 2)
    loads = [
        pltpu.make_async_copy(bx2.at[pl.ds(side * n, n)], cols.at[side, 2, pl.ds(n, n)], sems.at[side])
        for side in range(2)
    ]
    for load in loads:
        load.start()

    def lse_of(block):
        at = lax.rem(block + count, count) * SPANS
        v = [got[at + s] for s in range(SPANS)]
        top = jnp.maximum(jnp.maximum(v[0], v[1]), jnp.maximum(v[2], v[3]))
        return top + jnp.log(sum(jnp.exp(a - top) for a in v))

    fill_columns(cols, 0, odd, own, ab, b2, pc)
    fill_columns(cols, 1, odd, x, abx, None, pcx)
    mine = lse_of(b)
    image_lse[...] = mine[0]
    text_lse[...] = mine[SPANS]
    turned = mine.T
    for side in range(2):
        half = slice(n, 2 * n) if side == 0 else slice(0, n)
        rows[side, :n] = own[half]
        rows[side, n:] = core[half]
        at = SPANS * side
        row_lse = jnp.concatenate([turned[:, at : at + 1], turned[:, at + 1 : at + 2]])
        steps = (0, -2, -1 - 2 * odd, -3 + 2 * odd) if side == 0 else (0, 2, 3 - 2 * odd, 1 + 2 * odd)
        at = SPANS * (1 - side)
        for k in (0, 1, 3, 2):
            if k == 2:
                loads[side].wait()
            l = mine if k == 0 else lse_of(b + steps[k])
            col_lse = jnp.concatenate([l[at : at + 1], l[at + 2 : at + 3]], axis=1)
            s = dot_t(rows[side], cols[side, k]) * LOGIT_SCALE
            w = 0.5 * (jnp.exp(s - row_lse) + jnp.exp(s - col_lse))
            if k == 0:
                i = lax.broadcasted_iota(jnp.int32, s.shape, 0)
                j = lax.broadcasted_iota(jnp.int32, s.shape, 1)
                w = w - ((i == j) & (i < n)).astype(F32)
            weights[side, :, k * 2 * n : (k + 1) * 2 * n] = w.astype(BF16)
        total = LOGIT_SCALE * jnp.dot(
            weights[side], cols[side].reshape(STEPS * 2 * n, cols.shape[-1]), preferred_element_type=F32
        )
        kept[side] = total[:n]
        sent[side] = total[n:]


def add_kernel(kept, got, image_grad, text_grad):
    image_grad[...] = kept[0] + got[0]
    text_grad[...] = kept[1] + got[1]


def body(image_embeds, text_embeds):
    n, width = image_embeds.shape
    count = lax.axis_size("batch")
    assert count % 2 == 0
    piece = jax.ShapeDtypeStruct((n, width), BF16)
    i0, t0 = image_embeds.astype(BF16), text_embeds.astype(BF16)
    own, for_pair, for_across = call(
        pack_kernel, (jax.ShapeDtypeStruct((2 * n, width), BF16), piece, piece), [], 0, i0, t0
    )
    a_t, a_i = along(t0, 2), along(i0, -2)
    pair, across = in_pair(for_pair), across_pairs(for_across)
    ab, pc = jnp.concatenate([a_t, a_i]), jnp.concatenate([pair, across])
    b2 = in_pair(ab)
    core = over_core(own)
    x = over_x(own)
    corex = over_core(x)
    far_ab, far_pc = over_x(ab), over_x(pc)
    far_b = in_pair(far_ab)
    part = call(
        stats_kernel,
        jax.ShapeDtypeStruct((2, SPANS * n), F32),
        [pltpu.VMEM((2, SPANS * n, width), BF16), pltpu.VMEM((2, STEPS - 1, n, width), BF16)],
        4 * SPANS * n * (STEPS - 1) * n * width,
        own, core, x, corex, ab, pc,
    )
    seen = over_core(pc)
    far_ab, part = lax.optimization_barrier((far_ab, part))
    send = call(
        functools.partial(finish_kernel, count),
        jax.ShapeDtypeStruct((count * SPANS, 2 * SPANS, n), F32),
        [pltpu.VMEM((2, SPANS * n, width), BF16)],
        4 * SPANS * n * n * width,
        part, own, core, x, corex, b2, seen, remote=(6,),
    )
    got = lax.all_to_all(send, AXES, 0, 0, tiled=True)
    row = jax.ShapeDtypeStruct((n,), F32)
    both = jax.ShapeDtypeStruct((2, n, width), F32)
    image_lse, text_lse, kept, sent = call(
        functools.partial(grad_kernel, count),
        (row, row, both, both),
        [
            pltpu.VMEM((2, 2 * n, width), BF16),
            pltpu.VMEM((2, STEPS, 2 * n, width), BF16),
            pltpu.VMEM((2, 2 * n, STEPS * 2 * n), BF16),
            pltpu.SemaphoreType.DMA((2,)),
        ],
        8 * 2 * n * STEPS * 2 * n * width,
        got, own, core, x, ab, b2, pc, far_ab, far_b, far_pc, remote=(8,),
    )
    grad = jax.ShapeDtypeStruct((n, width), F32)
    image_grad, text_grad = call(add_kernel, (grad, grad), [], 0, kept, over_core(sent))
    return (image_lse, text_lse, image_grad, text_grad)


def solution(mesh):
    in_specs = (P(("batch", "span"), None), P(("batch", "span"), None))
    out_specs = (
        P(("batch", "span")),
        P(("batch", "span")),
        P(("batch", "span"), None),
        P(("batch", "span"), None),
    )
    return jax.shard_map(body, mesh=mesh, in_specs=in_specs, out_specs=out_specs, check_vma=False)
```

```python
import functools

import jax
import jax.numpy as jnp
from jax import lax
from jax.experimental import pallas as pl
from jax.experimental.pallas import tpu as pltpu
from jax.sharding import PartitionSpec as P

STEPS = 4
LOGIT_SCALE = 5.0
AXES = ("batch", "span")
SPANS = 4
F32, BF16 = jnp.float32, jnp.bfloat16
VMEM_LIMIT = 16 * 1024 * 1024


def moved(value, target):
    count, spans = lax.axis_size("batch"), lax.axis_size("span")
    pairs = []
    for b in range(count):
        for s in range(spans):
            to_b, to_s = target(b, s)
            pairs.append((b * spans + s, (to_b % count) * spans + to_s))
    return lax.ppermute(value, AXES, pairs)


def over_core(value):
    return moved(value, lambda b, s: (b, s ^ 1))


def over_x(value):
    return moved(value, lambda b, s: (b, s ^ 2))


def along(value, steps):
    return moved(value, lambda b, s: (b + steps, s))


def in_pair(value):
    return moved(value, lambda b, s: (b ^ 1, s))


def across_pairs(value):
    return moved(value, lambda b, s: (b + (3 if b % 2 else -3), s))


def after(value, first):
    return lax.optimization_barrier((value, first))[0]


def dot_t(a, b):
    return lax.dot_general(a, b, (((1,), (1,)), ((), ())), preferred_element_type=F32)


def call(kernel, out_shape, scratch, flops, *args, remote=()):
    whole = pl.BlockSpec(memory_space=pltpu.VMEM)
    size = sum(a.size * a.dtype.itemsize for a in args)
    return pl.pallas_call(
        kernel,
        out_shape=out_shape,
        in_specs=[pl.BlockSpec(memory_space=pl.ANY) if i in remote else whole for i in range(len(args))],
        out_specs=jax.tree.map(lambda _: whole, out_shape),
        scratch_shapes=scratch,
        compiler_params=pltpu.CompilerParams(vmem_limit_bytes=VMEM_LIMIT),
        cost_estimate=pl.CostEstimate(flops=flops, bytes_accessed=size, transcendentals=0),
    )(*args)


def pack_kernel(image, text, own, for_pair, for_across):
    n = image.shape[0]
    odd = lax.rem(lax.axis_index("batch"), 2)
    own[:n] = text[...]
    own[n:] = image[...]

    @pl.when(odd == 0)
    def _():
        for_pair[...] = text[...]
        for_across[...] = image[...]

    @pl.when(odd == 1)
    def _():
        for_pair[...] = image[...]
        for_across[...] = text[...]


def fill_columns(cols, place, odd, own, ab, b, pc):
    n = own.shape[0] // 2
    at = slice(place * n, (place + 1) * n)
    for side in range(2):
        for slot, ref in enumerate((own, ab, b)):
            if ref is not None:
                cols[side, slot, at] = ref[side * n : (side + 1) * n]
    cols[1 - odd, 3, at] = pc[:n]
    cols[odd, 3, at] = pc[n:]


def stats_kernel(own, core, x, corex, ab, pc, part, rows, cols):
    n = own.shape[0] // 2
    odd = lax.rem(lax.axis_index("batch"), 2)
    for side in range(2):
        for q, ref in enumerate((own, core, x, corex)):
            rows[side, q * n : (q + 1) * n] = ref[n:] if side == 0 else ref[:n]
        for slot, ref in enumerate((own, ab)):
            cols[side, slot] = ref[side * n : (side + 1) * n]
    cols[1 - odd, 2] = pc[:n]
    cols[odd, 2] = pc[n:]
    for side in range(2):
        s = dot_t(cols[side].reshape((STEPS - 1) * n, cols.shape[-1]), rows[side]) * LOGIT_SCALE
        top = jnp.max(s, axis=0, keepdims=True)
        part[side] = (top + jnp.log(jnp.sum(jnp.exp(s - top), axis=0, keepdims=True)))[0]


def finish_kernel(count, part, own, core, x, corex, b2, _, out, rows):
    n = own.shape[0] // 2
    pos = lax.axis_index("span")
    done = []
    for side in range(2):
        for q, ref in enumerate((own, core, x, corex)):
            rows[side, q * n : (q + 1) * n] = ref[n:] if side == 0 else ref[:n]
        s = dot_t(b2[side * n : (side + 1) * n], rows[side]) * LOGIT_SCALE
        before = part[side : side + 1]
        top = jnp.maximum(before, jnp.max(s, axis=0, keepdims=True))
        lse = top + jnp.log(jnp.exp(before - top) + jnp.sum(jnp.exp(s - top), axis=0, keepdims=True))
        done += [lse[:, q * n : (q + 1) * n] for q in range(SPANS)]
    for sigma in range(SPANS):
        v = jnp.concatenate([done[4 * (r // 4) + ((r % 4) ^ sigma)] for r in range(2 * SPANS)])
        to = pos ^ sigma

        def store(b, _):
            out[b * SPANS + to] = v
            return 0

        lax.fori_loop(0, count, store, 0)


def grad_kernel(count, *refs):
    got, own, core, x, ab, b2, pc, abx, bx2, pcx = refs[:10]
    image_lse, text_lse, kept, sent, rows, cols, weights, sems = refs[10:]
    n = own.shape[0] // 2
    b = lax.axis_index("batch")
    odd = lax.rem(b, 2)
    loads = [
        pltpu.make_async_copy(bx2.at[pl.ds(side * n, n)], cols.at[side, 2, pl.ds(n, n)], sems.at[side])
        for side in range(2)
    ]
    for load in loads:
        load.start()

    def lse_of(block):
        at = lax.rem(block + count, count) * SPANS
        v = [got[at + s] for s in range(SPANS)]
        top = jnp.maximum(jnp.maximum(v[0], v[1]), jnp.maximum(v[2], v[3]))
        return top + jnp.log(sum(jnp.exp(a - top) for a in v))

    fill_columns(cols, 0, odd, own, ab, b2, pc)
    fill_columns(cols, 1, odd, x, abx, None, pcx)
    mine = lse_of(b)
    image_lse[...] = mine[0]
    text_lse[...] = mine[SPANS]
    turned = mine.T
    for side in range(2):
        half = slice(n, 2 * n) if side == 0 else slice(0, n)
        rows[side, :n] = own[half]
        rows[side, n:] = core[half]
        at = SPANS * side
        row_lse = jnp.concatenate([turned[:, at : at + 1], turned[:, at + 1 : at + 2]])
        steps = (0, -2, -1 - 2 * odd, -3 + 2 * odd) if side == 0 else (0, 2, 3 - 2 * odd, 1 + 2 * odd)
        at = SPANS * (1 - side)
        for k in (0, 1, 3, 2):
            if k == 2:
                loads[side].wait()
            l = mine if k == 0 else lse_of(b + steps[k])
            col_lse = jnp.concatenate([l[at : at + 1], l[at + 2 : at + 3]], axis=1)
            s = dot_t(rows[side], cols[side, k]) * LOGIT_SCALE
            w = 0.5 * (jnp.exp(s - row_lse) + jnp.exp(s - col_lse))
            if k == 0:
                i = lax.broadcasted_iota(jnp.int32, s.shape, 0)
                j = lax.broadcasted_iota(jnp.int32, s.shape, 1)
                w = w - ((i == j) & (i < n)).astype(F32)
            weights[side, :, k * 2 * n : (k + 1) * 2 * n] = w.astype(BF16)
        total = LOGIT_SCALE * jnp.dot(
            weights[side], cols[side].reshape(STEPS * 2 * n, cols.shape[-1]), preferred_element_type=F32
        )
        kept[side] = total[:n]
        sent[side] = total[n:]


def add_kernel(kept, got, image_grad, text_grad):
    image_grad[...] = kept[0] + got[0]
    text_grad[...] = kept[1] + got[1]


def body(image_embeds, text_embeds):
    n, width = image_embeds.shape
    count = lax.axis_size("batch")
    assert count % 2 == 0
    piece = jax.ShapeDtypeStruct((n, width), BF16)
    i0, t0 = image_embeds.astype(BF16), text_embeds.astype(BF16)
    own, for_pair, for_across = call(
        pack_kernel, (jax.ShapeDtypeStruct((2 * n, width), BF16), piece, piece), [], 0, i0, t0
    )
    a_t, a_i = along(t0, 2), along(i0, -2)
    pair, across = in_pair(for_pair), across_pairs(for_across)
    ab, pc = jnp.concatenate([a_t, a_i]), jnp.concatenate([pair, across])
    b2 = in_pair(ab)
    core = over_core(own)
    x = over_x(own)
    corex = over_core(x)
    far_ab, far_pc = over_x(ab), over_x(pc)
    part = call(
        stats_kernel,
        jax.ShapeDtypeStruct((2, SPANS * n), F32),
        [pltpu.VMEM((2, SPANS * n, width), BF16), pltpu.VMEM((2, STEPS - 1, n, width), BF16)],
        4 * SPANS * n * (STEPS - 1) * n * width,
        own, core, x, corex, ab, pc,
    )
    seen = over_core(pc)
    far_ab, part = lax.optimization_barrier((far_ab, part))
    send = call(
        functools.partial(finish_kernel, count),
        jax.ShapeDtypeStruct((count * SPANS, 2 * SPANS, n), F32),
        [pltpu.VMEM((2, SPANS * n, width), BF16)],
        4 * SPANS * n * n * width,
        part, own, core, x, corex, b2, seen, remote=(6,),
    )
    far_b = in_pair(after(far_ab, send))
    got = lax.all_to_all(send, AXES, 0, 0, tiled=True)
    row = jax.ShapeDtypeStruct((n,), F32)
    both = jax.ShapeDtypeStruct((2, n, width), F32)
    image_lse, text_lse, kept, sent = call(
        functools.partial(grad_kernel, count),
        (row, row, both, both),
        [
            pltpu.VMEM((2, 2 * n, width), BF16),
            pltpu.VMEM((2, STEPS, 2 * n, width), BF16),
            pltpu.VMEM((2, 2 * n, STEPS * 2 * n), BF16),
            pltpu.SemaphoreType.DMA((2,)),
        ],
        8 * 2 * n * STEPS * 2 * n * width,
        got, own, core, x, ab, b2, pc, far_ab, far_b, far_pc, remote=(8,),
    )
    grad = jax.ShapeDtypeStruct((n, width), F32)
    image_grad, text_grad = call(add_kernel, (grad, grad), [], 0, kept, over_core(sent))
    return (image_lse, text_lse, image_grad, text_grad)


def solution(mesh):
    in_specs = (P(("batch", "span"), None), P(("batch", "span"), None))
    out_specs = (
        P(("batch", "span")),
        P(("batch", "span")),
        P(("batch", "span"), None),
        P(("batch", "span"), None),
    )
    return jax.shard_map(body, mesh=mesh, in_specs=in_specs, out_specs=out_specs, check_vma=False)
```

```python
import functools

import jax
import jax.numpy as jnp
from jax import lax
from jax.experimental import pallas as pl
from jax.experimental.pallas import tpu as pltpu
from jax.sharding import PartitionSpec as P

STEPS = 4
LOGIT_SCALE = 5.0
AXES = ("batch", "span")
SPANS = 4
F32, BF16 = jnp.float32, jnp.bfloat16
VMEM_LIMIT = 16 * 1024 * 1024


def moved(value, target):
    count, spans = lax.axis_size("batch"), lax.axis_size("span")
    pairs = []
    for b in range(count):
        for s in range(spans):
            to_b, to_s = target(b, s)
            pairs.append((b * spans + s, (to_b % count) * spans + to_s))
    return lax.ppermute(value, AXES, pairs)


def over_core(value):
    return moved(value, lambda b, s: (b, s ^ 1))


def over_x(value):
    return moved(value, lambda b, s: (b, s ^ 2))


def along(value, steps):
    return moved(value, lambda b, s: (b + steps, s))


def in_pair(value):
    return moved(value, lambda b, s: (b ^ 1, s))


def across_pairs(value):
    return moved(value, lambda b, s: (b + (3 if b % 2 else -3), s))


def after(value, first):
    return lax.optimization_barrier((value, first))[0]


def dot_t(a, b):
    return lax.dot_general(a, b, (((1,), (1,)), ((), ())), preferred_element_type=F32)


def call(kernel, out_shape, scratch, flops, *args, remote=()):
    whole = pl.BlockSpec(memory_space=pltpu.VMEM)
    size = sum(a.size * a.dtype.itemsize for a in args)
    return pl.pallas_call(
        kernel,
        out_shape=out_shape,
        in_specs=[pl.BlockSpec(memory_space=pl.ANY) if i in remote else whole for i in range(len(args))],
        out_specs=jax.tree.map(lambda _: whole, out_shape),
        scratch_shapes=scratch,
        compiler_params=pltpu.CompilerParams(vmem_limit_bytes=VMEM_LIMIT),
        cost_estimate=pl.CostEstimate(flops=flops, bytes_accessed=size, transcendentals=0),
    )(*args)


def pack_kernel(image, text, own, for_pair, for_across):
    n = image.shape[0]
    odd = lax.rem(lax.axis_index("batch"), 2)
    own[:n] = text[...]
    own[n:] = image[...]

    @pl.when(odd == 0)
    def _():
        for_pair[...] = text[...]
        for_across[...] = image[...]

    @pl.when(odd == 1)
    def _():
        for_pair[...] = image[...]
        for_across[...] = text[...]


def fill_columns(cols, place, odd, own, ab, b, pc):
    n = own.shape[0] // 2
    at = slice(place * n, (place + 1) * n)
    for side in range(2):
        for slot, ref in enumerate((own, ab, b)):
            if ref is not None:
                cols[side, slot, at] = ref[side * n : (side + 1) * n]
    cols[1 - odd, 3, at] = pc[:n]
    cols[odd, 3, at] = pc[n:]


def stats_kernel(own, core, x, corex, ab, pc, part, rows, cols):
    n = own.shape[0] // 2
    odd = lax.rem(lax.axis_index("batch"), 2)
    for side in range(2):
        for q, ref in enumerate((own, core, x, corex)):
            rows[side, q * n : (q + 1) * n] = ref[n:] if side == 0 else ref[:n]
        for slot, ref in enumerate((own, ab)):
            cols[side, slot] = ref[side * n : (side + 1) * n]
    cols[1 - odd, 2] = pc[:n]
    cols[odd, 2] = pc[n:]
    for side in range(2):
        s = dot_t(cols[side].reshape((STEPS - 1) * n, cols.shape[-1]), rows[side]) * LOGIT_SCALE
        top = jnp.max(s, axis=0, keepdims=True)
        part[side] = (top + jnp.log(jnp.sum(jnp.exp(s - top), axis=0, keepdims=True)))[0]


def finish_kernel(count, part, own, core, x, corex, b2, _, out, rows):
    n = own.shape[0] // 2
    pos = lax.axis_index("span")
    done = []
    for side in range(2):
        for q, ref in enumerate((own, core, x, corex)):
            rows[side, q * n : (q + 1) * n] = ref[n:] if side == 0 else ref[:n]
        s = dot_t(b2[side * n : (side + 1) * n], rows[side]) * LOGIT_SCALE
        before = part[side : side + 1]
        top = jnp.maximum(before, jnp.max(s, axis=0, keepdims=True))
        lse = top + jnp.log(jnp.exp(before - top) + jnp.sum(jnp.exp(s - top), axis=0, keepdims=True))
        done += [lse[:, q * n : (q + 1) * n] for q in range(SPANS)]
    for sigma in range(SPANS):
        v = jnp.concatenate([done[4 * (r // 4) + ((r % 4) ^ sigma)] for r in range(2 * SPANS)])
        to = pos ^ sigma

        def store(b, _):
            out[b * SPANS + to] = v
            return 0

        lax.fori_loop(0, count, store, 0)


def grad_kernel(count, *refs):
    got, own, core, x, ab, b2, pc, abx, bx2, pcx = refs[:10]
    image_lse, text_lse, kept, sent, rows, cols, weights, sems = refs[10:]
    n = own.shape[0] // 2
    b = lax.axis_index("batch")
    odd = lax.rem(b, 2)
    loads = [
        pltpu.make_async_copy(bx2.at[pl.ds(side * n, n)], cols.at[side, 2, pl.ds(n, n)], sems.at[side])
        for side in range(2)
    ]
    for load in loads:
        load.start()

    def lse_of(block):
        at = lax.rem(block + count, count) * SPANS
        v = [got[at + s] for s in range(SPANS)]
        top = jnp.maximum(jnp.maximum(v[0], v[1]), jnp.maximum(v[2], v[3]))
        return top + jnp.log(sum(jnp.exp(a - top) for a in v))

    fill_columns(cols, 0, odd, own, ab, b2, pc)
    fill_columns(cols, 1, odd, x, abx, None, pcx)
    mine = lse_of(b)
    image_lse[...] = mine[0]
    text_lse[...] = mine[SPANS]
    turned = mine.T
    for side in range(2):
        half = slice(n, 2 * n) if side == 0 else slice(0, n)
        rows[side, :n] = own[half]
        rows[side, n:] = core[half]
        at = SPANS * side
        row_lse = jnp.concatenate([turned[:, at : at + 1], turned[:, at + 1 : at + 2]])
        steps = (0, -2, -1 - 2 * odd, -3 + 2 * odd) if side == 0 else (0, 2, 3 - 2 * odd, 1 + 2 * odd)
        at = SPANS * (1 - side)
        for k in (0, 1, 3, 2):
            if k == 2:
                loads[side].wait()
            l = mine if k == 0 else lse_of(b + steps[k])
            col_lse = jnp.concatenate([l[at : at + 1], l[at + 2 : at + 3]], axis=1)
            s = dot_t(rows[side], cols[side, k]) * LOGIT_SCALE
            w = 0.5 * (jnp.exp(s - row_lse) + jnp.exp(s - col_lse))
            if k == 0:
                i = lax.broadcasted_iota(jnp.int32, s.shape, 0)
                j = lax.broadcasted_iota(jnp.int32, s.shape, 1)
                w = w - ((i == j) & (i < n)).astype(F32)
            weights[side, :, k * 2 * n : (k + 1) * 2 * n] = w.astype(BF16)
        total = LOGIT_SCALE * jnp.dot(
            weights[side], cols[side].reshape(STEPS * 2 * n, cols.shape[-1]), preferred_element_type=F32
        )
        kept[side] = total[:n]
        sent[side] = total[n:].astype(BF16)


def add_kernel(kept, got, image_grad, text_grad):
    image_grad[...] = kept[0] + got[0].astype(F32)
    text_grad[...] = kept[1] + got[1].astype(F32)


def body(image_embeds, text_embeds):
    n, width = image_embeds.shape
    count = lax.axis_size("batch")
    assert count % 2 == 0
    piece = jax.ShapeDtypeStruct((n, width), BF16)
    i0, t0 = image_embeds.astype(BF16), text_embeds.astype(BF16)
    own, for_pair, for_across = call(
        pack_kernel, (jax.ShapeDtypeStruct((2 * n, width), BF16), piece, piece), [], 0, i0, t0
    )
    a_t, a_i = along(t0, 2), along(i0, -2)
    pair, across = in_pair(for_pair), across_pairs(for_across)
    ab, pc = jnp.concatenate([a_t, a_i]), jnp.concatenate([pair, across])
    b2 = in_pair(ab)
    core = over_core(own)
    x = over_x(own)
    corex = over_core(x)
    far_ab, far_pc = over_x(ab), over_x(pc)
    part = call(
        stats_kernel,
        jax.ShapeDtypeStruct((2, SPANS * n), F32),
        [pltpu.VMEM((2, SPANS * n, width), BF16), pltpu.VMEM((2, STEPS - 1, n, width), BF16)],
        4 * SPANS * n * (STEPS - 1) * n * width,
        own, core, x, corex, ab, pc,
    )
    seen = over_core(pc)
    far_ab, part = lax.optimization_barrier((far_ab, part))
    send = call(
        functools.partial(finish_kernel, count),
        jax.ShapeDtypeStruct((count * SPANS, 2 * SPANS, n), F32),
        [pltpu.VMEM((2, SPANS * n, width), BF16)],
        4 * SPANS * n * n * width,
        part, own, core, x, corex, b2, seen, remote=(6,),
    )
    far_b = in_pair(after(far_ab, send))
    got = lax.all_to_all(send, AXES, 0, 0, tiled=True)
    row = jax.ShapeDtypeStruct((n,), F32)
    both = jax.ShapeDtypeStruct((2, n, width), F32)
    image_lse, text_lse, kept, sent = call(
        functools.partial(grad_kernel, count),
        (row, row, both, jax.ShapeDtypeStruct((2, n, width), BF16)),
        [
            pltpu.VMEM((2, 2 * n, width), BF16),
            pltpu.VMEM((2, STEPS, 2 * n, width), BF16),
            pltpu.VMEM((2, 2 * n, STEPS * 2 * n), BF16),
            pltpu.SemaphoreType.DMA((2,)),
        ],
        8 * 2 * n * STEPS * 2 * n * width,
        got, own, core, x, ab, b2, pc, far_ab, far_b, far_pc, remote=(8,),
    )
    grad = jax.ShapeDtypeStruct((n, width), F32)
    image_grad, text_grad = call(add_kernel, (grad, grad), [], 0, kept, over_core(sent))
    return (image_lse, text_lse, image_grad, text_grad)


def solution(mesh):
    in_specs = (P(("batch", "span"), None), P(("batch", "span"), None))
    out_specs = (
        P(("batch", "span")),
        P(("batch", "span")),
        P(("batch", "span"), None),
        P(("batch", "span"), None),
    )
    return jax.shard_map(body, mesh=mesh, in_specs=in_specs, out_specs=out_specs, check_vma=False)
```

```python
import functools

import jax
import jax.numpy as jnp
from jax import lax
from jax.experimental import pallas as pl
from jax.experimental.pallas import tpu as pltpu
from jax.sharding import PartitionSpec as P

STEPS = 4
LOGIT_SCALE = 5.0
AXES = ("batch", "span")
SPANS = 4
F32, BF16 = jnp.float32, jnp.bfloat16
VMEM_LIMIT = 16 * 1024 * 1024


def moved(value, target):
    count, spans = lax.axis_size("batch"), lax.axis_size("span")
    pairs = []
    for b in range(count):
        for s in range(spans):
            to_b, to_s = target(b, s)
            pairs.append((b * spans + s, (to_b % count) * spans + to_s))
    return lax.ppermute(value, AXES, pairs)


def over_core(value):
    return moved(value, lambda b, s: (b, s ^ 1))


def over_x(value):
    return moved(value, lambda b, s: (b, s ^ 2))


def along(value, steps):
    return moved(value, lambda b, s: (b + steps, s))


def in_pair(value):
    return moved(value, lambda b, s: (b ^ 1, s))


def across_pairs(value):
    return moved(value, lambda b, s: (b + (3 if b % 2 else -3), s))


def after(value, first):
    return lax.optimization_barrier((value, first))[0]


def dot_t(a, b):
    return lax.dot_general(a, b, (((1,), (1,)), ((), ())), preferred_element_type=F32)


def call(kernel, out_shape, scratch, flops, *args, remote=()):
    whole = pl.BlockSpec(memory_space=pltpu.VMEM)
    size = sum(a.size * a.dtype.itemsize for a in args)
    return pl.pallas_call(
        kernel,
        out_shape=out_shape,
        in_specs=[pl.BlockSpec(memory_space=pl.ANY) if i in remote else whole for i in range(len(args))],
        out_specs=jax.tree.map(lambda _: whole, out_shape),
        scratch_shapes=scratch,
        compiler_params=pltpu.CompilerParams(vmem_limit_bytes=VMEM_LIMIT),
        cost_estimate=pl.CostEstimate(flops=flops, bytes_accessed=size, transcendentals=0),
    )(*args)


def pack_kernel(image, text, own, for_pair, for_across):
    n = image.shape[0]
    odd = lax.rem(lax.axis_index("batch"), 2)
    own[:n] = text[...]
    own[n:] = image[...]

    @pl.when(odd == 0)
    def _():
        for_pair[...] = text[...]
        for_across[...] = image[...]

    @pl.when(odd == 1)
    def _():
        for_pair[...] = image[...]
        for_across[...] = text[...]


def fill_columns(cols, place, odd, own, ab, b, pc):
    n = own.shape[0] // 2
    at = slice(place * n, (place + 1) * n)
    for side in range(2):
        for slot, ref in enumerate((own, ab, b)):
            if ref is not None:
                cols[side, slot, at] = ref[side * n : (side + 1) * n]
    cols[1 - odd, 3, at] = pc[:n]
    cols[odd, 3, at] = pc[n:]


def stats_kernel(own, core, x, corex, ab, pc, part, rows, cols):
    n = own.shape[0] // 2
    odd = lax.rem(lax.axis_index("batch"), 2)
    for side in range(2):
        for q, ref in enumerate((own, core, x, corex)):
            rows[side, q * n : (q + 1) * n] = ref[n:] if side == 0 else ref[:n]
        for slot, ref in enumerate((own, ab)):
            cols[side, slot] = ref[side * n : (side + 1) * n]
    cols[1 - odd, 2] = pc[:n]
    cols[odd, 2] = pc[n:]
    for side in range(2):
        s = dot_t(cols[side].reshape((STEPS - 1) * n, cols.shape[-1]), rows[side]) * LOGIT_SCALE
        top = jnp.max(s, axis=0, keepdims=True)
        part[side] = (top + jnp.log(jnp.sum(jnp.exp(s - top), axis=0, keepdims=True)))[0]


def finish_kernel(count, part, own, core, x, corex, b2, _, out):
    n = own.shape[0] // 2
    pos = lax.axis_index("span")
    done = []
    for side in range(2):
        half = slice(n, 2 * n) if side == 0 else slice(0, n)
        rows = jnp.concatenate([ref[half] for ref in (own, core, x, corex)])
        s = dot_t(b2[side * n : (side + 1) * n], rows) * LOGIT_SCALE
        before = part[side : side + 1]
        top = jnp.maximum(before, jnp.max(s, axis=0, keepdims=True))
        lse = top + jnp.log(jnp.exp(before - top) + jnp.sum(jnp.exp(s - top), axis=0, keepdims=True))
        done += [lse[:, q * n : (q + 1) * n] for q in range(SPANS)]
    for sigma in range(SPANS):
        v = jnp.concatenate([done[4 * (r // 4) + ((r % 4) ^ sigma)] for r in range(2 * SPANS)])
        to = pos ^ sigma

        def store(b, _):
            out[b * SPANS + to] = v
            return 0

        lax.fori_loop(0, count, store, 0, unroll=count <= 16)


def grad_kernel(count, *refs):
    got, own, core, x, ab, b2, pc, abx, bx2, pcx = refs[:10]
    image_lse, text_lse, kept, sent, rows, cols, weights, sems = refs[10:]
    n = own.shape[0] // 2
    b = lax.axis_index("batch")
    odd = lax.rem(b, 2)
    loads = [
        pltpu.make_async_copy(bx2.at[pl.ds(side * n, n)], cols.at[side, 2, pl.ds(n, n)], sems.at[side])
        for side in range(2)
    ]
    for load in loads:
        load.start()

    def lse_of(block):
        at = lax.rem(block + count, count) * SPANS
        v = [got[at + s] for s in range(SPANS)]
        top = jnp.maximum(jnp.maximum(v[0], v[1]), jnp.maximum(v[2], v[3]))
        return top + jnp.log(sum(jnp.exp(a - top) for a in v))

    fill_columns(cols, 0, odd, own, ab, b2, pc)
    fill_columns(cols, 1, odd, x, abx, None, pcx)
    mine = lse_of(b)
    image_lse[...] = mine[0]
    text_lse[...] = mine[SPANS]
    turned = mine.T
    for side in range(2):
        half = slice(n, 2 * n) if side == 0 else slice(0, n)
        rows[side, :n] = own[half]
        rows[side, n:] = core[half]
        at = SPANS * side
        row_lse = jnp.concatenate([turned[:, at : at + 1], turned[:, at + 1 : at + 2]])
        steps = (0, -2, -1 - 2 * odd, -3 + 2 * odd) if side == 0 else (0, 2, 3 - 2 * odd, 1 + 2 * odd)
        at = SPANS * (1 - side)
        for k in (0, 1, 3, 2):
            if k == 2:
                loads[side].wait()
            l = mine if k == 0 else lse_of(b + steps[k])
            col_lse = jnp.concatenate([l[at : at + 1], l[at + 2 : at + 3]], axis=1)
            s = dot_t(rows[side], cols[side, k]) * LOGIT_SCALE
            w = 0.5 * (jnp.exp(s - row_lse) + jnp.exp(s - col_lse))
            if k == 0:
                i = lax.broadcasted_iota(jnp.int32, s.shape, 0)
                j = lax.broadcasted_iota(jnp.int32, s.shape, 1)
                w = w - ((i == j) & (i < n)).astype(F32)
            weights[side, :, k * 2 * n : (k + 1) * 2 * n] = w.astype(BF16)
    for side in range(2):
        total = LOGIT_SCALE * jnp.dot(
            weights[side], cols[side].reshape(STEPS * 2 * n, cols.shape[-1]), preferred_element_type=F32
        )
        kept[side] = total[:n]
        sent[side] = total[n:].astype(BF16)


def add_kernel(kept, got, image_grad, text_grad):
    image_grad[...] = kept[0] + got[0].astype(F32)
    text_grad[...] = kept[1] + got[1].astype(F32)


def body(image_embeds, text_embeds):
    n, width = image_embeds.shape
    count = lax.axis_size("batch")
    assert count % 2 == 0
    piece = jax.ShapeDtypeStruct((n, width), BF16)
    i0, t0 = image_embeds.astype(BF16), text_embeds.astype(BF16)
    own, for_pair, for_across = call(
        pack_kernel, (jax.ShapeDtypeStruct((2 * n, width), BF16), piece, piece), [], 0, i0, t0
    )
    a_t, a_i = along(t0, 2), along(i0, -2)
    pair, across = in_pair(for_pair), across_pairs(for_across)
    ab, pc = jnp.concatenate([a_t, a_i]), jnp.concatenate([pair, across])
    b2 = in_pair(ab)
    core = over_core(own)
    x = over_x(own)
    corex = over_core(x)
    far_ab, far_pc = over_x(ab), over_x(pc)
    part = call(
        stats_kernel,
        jax.ShapeDtypeStruct((2, SPANS * n), F32),
        [pltpu.VMEM((2, SPANS * n, width), BF16), pltpu.VMEM((2, STEPS - 1, n, width), BF16)],
        4 * SPANS * n * (STEPS - 1) * n * width,
        own, core, x, corex, ab, pc,
    )
    seen = over_core(pc)
    far_ab, part = lax.optimization_barrier((far_ab, part))
    send = call(
        functools.partial(finish_kernel, count),
        jax.ShapeDtypeStruct((count * SPANS, 2 * SPANS, n), F32),
        [],
        4 * SPANS * n * n * width,
        part, own, core, x, corex, b2, seen, remote=(6,),
    )
    far_b = in_pair(after(far_ab, send))
    got = lax.all_to_all(send, AXES, 0, 0, tiled=True)
    row = jax.ShapeDtypeStruct((n,), F32)
    both = jax.ShapeDtypeStruct((2, n, width), F32)
    image_lse, text_lse, kept, sent = call(
        functools.partial(grad_kernel, count),
        (row, row, both, jax.ShapeDtypeStruct((2, n, width), BF16)),
        [
            pltpu.VMEM((2, 2 * n, width), BF16),
            pltpu.VMEM((2, STEPS, 2 * n, width), BF16),
            pltpu.VMEM((2, 2 * n, STEPS * 2 * n), BF16),
            pltpu.SemaphoreType.DMA((2,)),
        ],
        8 * 2 * n * STEPS * 2 * n * width,
        got, own, core, x, ab, b2, pc, far_ab, far_b, far_pc, remote=(8,),
    )
    grad = jax.ShapeDtypeStruct((n, width), F32)
    image_grad, text_grad = call(add_kernel, (grad, grad), [], 0, kept, over_core(sent))
    return (image_lse, text_lse, image_grad, text_grad)


def solution(mesh):
    in_specs = (P(("batch", "span"), None), P(("batch", "span"), None))
    out_specs = (
        P(("batch", "span")),
        P(("batch", "span")),
        P(("batch", "span"), None),
        P(("batch", "span"), None),
    )
    return jax.shard_map(body, mesh=mesh, in_specs=in_specs, out_specs=out_specs, check_vma=False)
```
